32 devices in a mesh: docs: 16 (over z, y, x), cols: 2 (over core).
Axes of the slice: x: 2, y: 2, z: 4, core: 2. Of those that a mesh axis runs over, the one named last changes fastest.
Arguments:
- blocks: bfloat16 [256, 64, 128, 128], P('docs', 'cols'), may hold values from -3 to 3
- slot_entry: int32 [256, 64], P('docs', 'cols'), may hold values from 0 to 63, as said below
- ghost_table: int32 [16, 2, 16, 4], P('docs', 'cols'), may hold values from 0 to 63, as said below
- live_counts: int32 [256, 2], P('docs', 'cols'), may hold values from 1 to 32, as said below
- test_matrix: bfloat16 [262144, 256], P(('docs', 'cols')), may hold values from -6 to 6
Outputs:
- basis_rows: bfloat16 [32768, 256], P('docs')
- projected: bfloat16 [256, 262144], P(None, ('docs', 'cols'))
The draws below stay inside these ranges and needn't reach their ends.
Inputs may be any that keep to these rules, and one draw needn't show every extreme that they name: `slot_entry`: the 32 entries of one block row in one half are distinct. `ghost_table`: for each d, c and o the 4 entries are distinct. `live_counts`: every index of docs has, in each half, a block row with all 32 slots live.
All inputs are finite; a program needn't handle non-finite values.
Results may differ from the reference program's by a relative error of at most 0.0055.
Values may be sent and summed in bfloat16 or wider, within the bound.
A program may use at most 256 MiB of HBM per device.

```python
import math
import jax
import jax.numpy as jnp
from jax import lax

EDGE = 128
RANK = 256
COL_BLOCKS = 64
SLOTS = 32
PER_OWNER = 4
BLOCK_ROWS = 16
ROW_BLOCKS = 256
DOCS = 32768
NGRAMS = 262144
N_DOCS = 16
N_COLS = 2


def draw_blocks(key, part):
    key = jax.random.fold_in(key, 11)
    keys = jax.random.split(key, 3)
    shape = (ROW_BLOCKS, N_COLS * SLOTS, EDGE, EDGE)
    row_scale = jnp.exp(jax.random.uniform(keys[0], (ROW_BLOCKS, 1, EDGE, 1), jnp.float32, 0.0, math.log(10.0)))
    col_scale = jnp.exp(jax.random.uniform(keys[1], (ROW_BLOCKS, N_COLS * SLOTS, 1, EDGE), jnp.float32, 0.0, math.log(10.0)))
    rise = 1.0 + 2.0 * jnp.arange(ROW_BLOCKS, dtype=jnp.float32).reshape(-1, 1, 1, 1) / max(ROW_BLOCKS - 1, 1)
    values = jnp.clip(jax.random.normal(keys[2], shape, jnp.float32), -4.0, 4.0)
    return (0.0025 * values * row_scale * col_scale * rise).astype(jnp.bfloat16)


def draw_slot_entry(key, part):
    key = jax.random.fold_in(key, 12)
    entries = N_DOCS * PER_OWNER
    scores = jax.random.randint(key, (ROW_BLOCKS, N_COLS, entries), 0, 1 << 16) * entries + jnp.arange(entries, dtype=jnp.int32)
    _, chosen = lax.top_k(scores, SLOTS)
    return chosen.astype(jnp.int32).reshape(ROW_BLOCKS, N_COLS * SLOTS)


def draw_ghost_table(key, part):
    key = jax.random.fold_in(key, 13)
    scores = jax.random.randint(key, (N_DOCS, N_COLS, N_DOCS, COL_BLOCKS), 0, 1 << 20) * COL_BLOCKS + jnp.arange(COL_BLOCKS, dtype=jnp.int32)
    _, chosen = lax.top_k(scores, PER_OWNER)
    return chosen.astype(jnp.int32)


def draw_live_counts(key, part):
    key = jax.random.fold_in(key, 14)
    keys = jax.random.split(key, 3)
    floor_level = jax.random.randint(keys[0], (N_DOCS, 1, N_COLS), 1, SLOTS // 2 + 1)
    spread = jax.random.randint(keys[1], (N_DOCS, BLOCK_ROWS, N_COLS), 0, 1 << 20)
    values = floor_level + spread % (SLOTS + 1 - floor_level)
    position = jax.random.randint(keys[2], (N_DOCS, 1, N_COLS), 0, BLOCK_ROWS)
    rows = jnp.arange(BLOCK_ROWS, dtype=jnp.int32)[None, :, None]
    values = jnp.where(rows == position, SLOTS, values)
    return values.astype(jnp.int32).reshape(ROW_BLOCKS, N_COLS)


def block_scale(own_key, shape, cuts, least, high):
    level = 1.0
    for axis_at, shards_of in cuts:
        heights = jax.random.uniform(jax.random.fold_in(jax.random.fold_in(own_key, 6), axis_at), (shards_of,), jnp.float32, least / len(cuts), high / len(cuts))
        level = level * jnp.repeat(jnp.exp(heights), shape[axis_at] // shards_of).reshape((-1,) + (1,) * (len(shape) - 1 - axis_at))
    return level


def centred(stream_key, extent, scale, reach, cuts=(), kind=jnp.bfloat16):
    drawn = scale * jax.random.normal(stream_key, extent, jnp.float32)
    if cuts:
        drawn = drawn * block_scale(stream_key, extent, cuts, -0.22, 0.18)
    return jnp.clip(drawn, -reach, reach).astype(kind)


def setup_inputs(seed: int = 0) -> dict:
    splits = jax.random.split(jax.random.key(seed), 6)
    return {
        "blocks": draw_blocks(jax.random.fold_in(splits[5], 71), 0),
        "slot_entry": draw_slot_entry(jax.random.fold_in(splits[5], 71), 0),
        "ghost_table": draw_ghost_table(jax.random.fold_in(splits[5], 71), 0),
        "live_counts": draw_live_counts(jax.random.fold_in(splits[5], 71), 0),
        "test_matrix": centred(splits[4], (NGRAMS, RANK), 1.0, 6.0, ((0, 32),)),
    }


def column_blocks(slot_entry, ghost_table):
    group_of = jnp.arange(ROW_BLOCKS, dtype=jnp.int32) // BLOCK_ROWS
    entries = slot_entry.reshape(ROW_BLOCKS, N_COLS, SLOTS)
    owner = entries // PER_OWNER
    within = entries % PER_OWNER
    halves = jnp.arange(N_COLS, dtype=jnp.int32)[None, :, None]
    local = ghost_table[group_of[:, None, None], halves, owner, within]
    return ((owner * N_COLS + halves) * COL_BLOCKS + local).reshape(ROW_BLOCKS, N_COLS * SLOTS)

def reference(blocks, slot_entry, ghost_table, live_counts, test_matrix):
    columns = column_blocks(slot_entry, ghost_table)
    slot_index = jnp.arange(N_COLS * SLOTS, dtype=jnp.int32)
    half_of = slot_index // SLOTS
    active = (slot_index[None, :] % SLOTS < live_counts[:, half_of]).astype(jnp.float32)
    pieces_all = test_matrix.reshape(-1, EDGE, RANK)
    group_blocks = blocks.reshape(N_DOCS, BLOCK_ROWS, N_COLS * SLOTS, EDGE, EDGE)
    group_columns = columns.reshape(N_DOCS, BLOCK_ROWS, N_COLS * SLOTS)
    group_active = active.reshape(N_DOCS, BLOCK_ROWS, N_COLS * SLOTS)

    def sketch_group(inputs):
        stored, chosen, weights = inputs
        pieces = pieces_all[chosen].astype(jnp.float32)
        masked = stored.astype(jnp.float32) * weights[:, :, None, None]
        return jnp.einsum('rsij,rsjk->rik', masked, pieces, precision=lax.Precision.HIGHEST)
    sketch = lax.map(sketch_group, (group_blocks, group_columns, group_active)).reshape(DOCS, RANK)
    gram = jnp.dot(sketch.T, sketch, precision=lax.Precision.HIGHEST)
    lower = jnp.linalg.cholesky(gram)
    solved = lax.linalg.triangular_solve(lower, sketch.T, left_side=True, lower=True)
    basis_rows = solved.T.astype(jnp.bfloat16)
    entries = N_DOCS * PER_OWNER
    segment = half_of[None, :] * entries + slot_entry
    group_segment = segment.reshape(N_DOCS, BLOCK_ROWS, N_COLS * SLOTS)
    entry_index = jnp.arange(entries, dtype=jnp.int32)
    owner_of = entry_index // PER_OWNER
    within_of = entry_index % PER_OWNER
    halves = jnp.arange(N_COLS, dtype=jnp.int32)[:, None]
    target = (owner_of[None, None, :] * N_COLS + halves[None, :, :]) * COL_BLOCKS + ghost_table[:, halves, owner_of[None, :], within_of[None, :]]
    group_basis = basis_rows.astype(jnp.float32).reshape(N_DOCS, BLOCK_ROWS, EDGE, RANK)

    def project_group(total, inputs):
        stored, weights, seg, rows, goal = inputs
        masked = stored.astype(jnp.float32) * weights[:, :, None, None]
        terms = jnp.einsum('rib,rsij->rsbj', rows, masked, precision=lax.Precision.HIGHEST)
        summed = jax.ops.segment_sum(terms.reshape(-1, RANK, EDGE), seg.reshape(-1), num_segments=N_COLS * entries)
        rounded = lax.optimization_barrier(summed.astype(jnp.bfloat16)).astype(jnp.float32)
        return (total.at[goal.reshape(-1)].add(rounded), None)
    start = jnp.zeros((NGRAMS // EDGE, RANK, EDGE), jnp.float32)
    total, _ = lax.scan(project_group, start, (group_blocks, group_active, group_segment, group_basis, target))
    projected = total.transpose(1, 0, 2).reshape(RANK, NGRAMS).astype(jnp.bfloat16)
    return (basis_rows, projected)
```

```python
import functools

import jax
import jax.numpy as jnp
from jax import lax
from jax.experimental import pallas as pl
from jax.experimental.pallas import tpu as pltpu
from jax.sharding import PartitionSpec as P

VMEM_BYTES = 60 * 1024 * 1024
SKETCH_GROUP = 8
PROJECT_GROUP = 4


def gram_of(rows_block):
    return lax.dot_general(
        rows_block, rows_block, (((0,), (0,)), ((), ())), precision=lax.Precision.HIGHEST
    )


def live_block(blocks_ref, k, live):
    stored = blocks_ref[0, k]
    return jnp.where(k < live, stored, jnp.zeros_like(stored))


def sketch_kernel(live_ref, entry_ref, blocks_ref, fetched_ref, out_ref):
    row = pl.program_id(0)
    live = live_ref[row]
    out_ref[...] = jnp.zeros_like(out_ref)

    def body(group, carry):
        first = group * SKETCH_GROUP
        slots = [first + i for i in range(SKETCH_GROUP)]
        stored = jnp.concatenate([live_block(blocks_ref, k, live) for k in slots], axis=1)
        pieces = jnp.concatenate([fetched_ref[entry_ref[row, k]] for k in slots], axis=0)
        out_ref[...] += jnp.dot(stored, pieces, preferred_element_type=jnp.float32)
        return carry

    lax.fori_loop(0, (live + SKETCH_GROUP - 1) // SKETCH_GROUP, body, 0)


def sketch_terms(live, slot_entry, blocks, fetched):
    block_rows, slots, edge, _ = blocks.shape
    width = fetched.shape[-1]
    return pl.pallas_call(
        sketch_kernel,
        out_shape=jax.ShapeDtypeStruct((block_rows * edge, width), jnp.float32),
        grid_spec=pltpu.PrefetchScalarGridSpec(
            num_scalar_prefetch=2,
            grid=(block_rows,),
            in_specs=[
                pl.BlockSpec((1, slots, edge, edge), lambda r, *_: (r, 0, 0, 0)),
                pl.BlockSpec(memory_space=pltpu.VMEM),
            ],
            out_specs=pl.BlockSpec((edge, width), lambda r, *_: (r, 0)),
        ),
        compiler_params=pltpu.CompilerParams(vmem_limit_bytes=VMEM_BYTES),
        name="sketch_terms",
    )(live, slot_entry, blocks, fetched)


def project_kernel(live_ref, entry_ref, blocks_ref, basis_ref, out_ref, total):
    row = pl.program_id(0)
    edge = blocks_ref.shape[-1]
    live = live_ref[row]

    @pl.when(row == 0)
    def _():
        @pl.loop(0, total.shape[0])
        def _(e):
            total[e] = jnp.zeros(total.shape[1:], total.dtype)

    basis = basis_ref[...]

    def body(group, carry):
        first = group * PROJECT_GROUP
        slots = [first + i for i in range(PROJECT_GROUP)]
        stored = jnp.concatenate([live_block(blocks_ref, k, live) for k in slots], axis=1)
        terms = jnp.dot(basis, stored, preferred_element_type=jnp.float32)
        for i, k in enumerate(slots):
            total[entry_ref[row, k]] += terms[:, i * edge : (i + 1) * edge]
        return carry

    lax.fori_loop(0, (live + PROJECT_GROUP - 1) // PROJECT_GROUP, body, 0)

    @pl.when(row == pl.num_programs(0) - 1)
    def _():
        @pl.loop(0, total.shape[0])
        def _(e):
            out_ref[e] = total[e].astype(out_ref.dtype)


def project_terms(live, slot_entry, blocks, basis, entries):
    block_rows, slots, edge, _ = blocks.shape
    width = basis.shape[0]
    return pl.pallas_call(
        project_kernel,
        out_shape=jax.ShapeDtypeStruct((entries, width, edge), jnp.bfloat16),
        grid_spec=pltpu.PrefetchScalarGridSpec(
            num_scalar_prefetch=2,
            grid=(block_rows,),
            in_specs=[
                pl.BlockSpec((1, slots, edge, edge), lambda r, *_: (r, 0, 0, 0)),
                pl.BlockSpec((width, edge), lambda r, *_: (0, r)),
            ],
            out_specs=pl.BlockSpec(memory_space=pltpu.VMEM),
            scratch_shapes=[pltpu.VMEM((entries, width, edge), jnp.float32)],
        ),
        compiler_params=pltpu.CompilerParams(vmem_limit_bytes=VMEM_BYTES),
        name="project_terms",
    )(live, slot_entry, blocks, basis)


def owner_sum_kernel(goal_ref, incoming_ref, out_ref, total):
    edge = incoming_ref.shape[-1]

    @pl.loop(0, total.shape[0])
    def _(b):
        total[b] = jnp.zeros(total.shape[1:], total.dtype)

    @pl.loop(0, incoming_ref.shape[0])
    def _(i):
        total[goal_ref[i]] += incoming_ref[i].astype(jnp.float32)

    for b in range(total.shape[0]):
        out_ref[:, b * edge : (b + 1) * edge] = total[b].astype(out_ref.dtype)


def owner_sum(goal, incoming, owned_blocks):
    _, width, edge = incoming.shape
    return pl.pallas_call(
        owner_sum_kernel,
        out_shape=jax.ShapeDtypeStruct((width, owned_blocks * edge), jnp.bfloat16),
        in_specs=[
            pl.BlockSpec(memory_space=pltpu.SMEM),
            pl.BlockSpec(memory_space=pltpu.VMEM),
        ],
        out_specs=pl.BlockSpec(memory_space=pltpu.VMEM),
        scratch_shapes=[pltpu.VMEM((owned_blocks, width, edge), jnp.float32)],
        compiler_params=pltpu.CompilerParams(vmem_limit_bytes=VMEM_BYTES),
        name="owner_sum",
    )(goal, incoming)


def docs_sum(value):
    owners = lax.axis_size("docs")
    step = 1
    while step < owners:
        value = value + lax.ppermute(value, "docs", [(i, i ^ step) for i in range(owners)])
        step *= 2
    return value


def on_device(blocks, slot_entry, ghost_table, live_counts, test_matrix):
    block_rows, slot_count, block_edge, _ = blocks.shape
    sketch_width = test_matrix.shape[1]
    owners = lax.axis_size("docs")
    table = ghost_table.reshape(owners, ghost_table.shape[-1])
    per_owner = table.shape[1]
    entries = owners * per_owner
    live = live_counts.reshape(block_rows)
    requests = lax.all_to_all(table, "docs", split_axis=0, concat_axis=0, tiled=True)
    local_pieces = test_matrix.reshape(-1, block_edge, sketch_width)
    fetched = lax.all_to_all(
        local_pieces[requests], "docs", split_axis=0, concat_axis=0, tiled=True
    )
    fetched = fetched.reshape(entries, block_edge, sketch_width)

    terms = sketch_terms(live, slot_entry, blocks, fetched)
    sketch = terms + lax.ppermute(terms, "cols", [(0, 1), (1, 0)])
    gram = docs_sum(gram_of(sketch))
    lower = jnp.linalg.cholesky(gram)
    basis = lax.linalg.triangular_solve(lower, sketch.T, left_side=True, lower=True)
    basis = basis.astype(jnp.bfloat16)
    basis_rows = basis.T

    outgoing = project_terms(live, slot_entry, blocks, basis, entries)
    incoming = lax.all_to_all(
        outgoing.reshape(owners, per_owner, sketch_width, block_edge),
        "docs", split_axis=0, concat_axis=0, tiled=True,
    )
    projected = owner_sum(
        requests.reshape(-1),
        incoming.reshape(-1, sketch_width, block_edge),
        test_matrix.shape[0] // block_edge,
    )
    return (basis_rows, projected)


def solution(mesh):
    in_specs = (
        P("docs", "cols", None, None),
        P("docs", "cols"),
        P("docs", "cols", None, None),
        P("docs", "cols"),
        P(("docs", "cols"), None),
    )
    out_specs = (P("docs", None), P(None, ("docs", "cols")))
    return jax.shard_map(
        on_device, mesh=mesh, in_specs=in_specs, out_specs=out_specs, check_vma=False
    )
```

```python
import jax
import jax.numpy as jnp
from jax import lax
from jax.experimental import pallas as pl
from jax.experimental.pallas import tpu as pltpu
from jax.sharding import PartitionSpec as P

VMEM_BYTES = 60 * 1024 * 1024
SKETCH_GROUP = 8
PROJECT_GROUP = 4


def gram_of(rows_block):
    return lax.dot_general(
        rows_block, rows_block, (((0,), (0,)), ((), ())), precision=lax.Precision.HIGHEST
    )


def live_block(blocks_ref, k, live):
    stored = blocks_ref[0, k]
    return jnp.where(k < live, stored, jnp.zeros_like(stored))


def sketch_kernel(live_ref, entry_ref, blocks_ref, fetched_ref, out_ref):
    row = pl.program_id(0)
    live = live_ref[row]
    out_ref[...] = jnp.zeros_like(out_ref)

    def body(group, carry):
        first = group * SKETCH_GROUP
        slots = [first + i for i in range(SKETCH_GROUP)]
        stored = jnp.concatenate([live_block(blocks_ref, k, live) for k in slots], axis=1)
        pieces = jnp.concatenate([fetched_ref[entry_ref[row, k]] for k in slots], axis=0)
        out_ref[...] += jnp.dot(stored, pieces, preferred_element_type=jnp.float32)
        return carry

    lax.fori_loop(0, (live + SKETCH_GROUP - 1) // SKETCH_GROUP, body, 0)


def sketch_terms(live, slot_entry, blocks, fetched):
    block_rows, slots, edge, _ = blocks.shape
    width = fetched.shape[-1]
    return pl.pallas_call(
        sketch_kernel,
        out_shape=jax.ShapeDtypeStruct((block_rows * edge, width), jnp.float32),
        grid_spec=pltpu.PrefetchScalarGridSpec(
            num_scalar_prefetch=2,
            grid=(block_rows,),
            in_specs=[
                pl.BlockSpec((1, slots, edge, edge), lambda r, *_: (r, 0, 0, 0)),
                pl.BlockSpec(memory_space=pltpu.VMEM),
            ],
            out_specs=pl.BlockSpec((edge, width), lambda r, *_: (r, 0)),
        ),
        compiler_params=pltpu.CompilerParams(vmem_limit_bytes=VMEM_BYTES),
        name="sketch_terms",
    )(live, slot_entry, blocks, fetched)


def project_kernel(live_ref, entry_ref, blocks_ref, basis_ref, out_ref, total):
    row = pl.program_id(0)
    edge = blocks_ref.shape[-1]
    live = live_ref[row]

    @pl.when(row == 0)
    def _():
        @pl.loop(0, total.shape[0])
        def _(e):
            total[e] = jnp.zeros(total.shape[1:], total.dtype)

    basis = basis_ref[...]

    def body(group, carry):
        first = group * PROJECT_GROUP
        slots = [first + i for i in range(PROJECT_GROUP)]
        stored = jnp.concatenate([live_block(blocks_ref, k, live) for k in slots], axis=1)
        terms = jnp.dot(basis, stored, preferred_element_type=jnp.float32)
        for i, k in enumerate(slots):
            total[entry_ref[row, k]] += terms[:, i * edge : (i + 1) * edge]
        return carry

    lax.fori_loop(0, (live + PROJECT_GROUP - 1) // PROJECT_GROUP, body, 0)

    @pl.when(row == pl.num_programs(0) - 1)
    def _():
        @pl.loop(0, total.shape[0])
        def _(e):
            out_ref[e] = total[e].astype(out_ref.dtype)


def project_terms(live, slot_entry, blocks, basis, entries):
    block_rows, slots, edge, _ = blocks.shape
    width = basis.shape[0]
    return pl.pallas_call(
        project_kernel,
        out_shape=jax.ShapeDtypeStruct((entries, width, edge), jnp.bfloat16),
        grid_spec=pltpu.PrefetchScalarGridSpec(
            num_scalar_prefetch=2,
            grid=(block_rows,),
            in_specs=[
                pl.BlockSpec((1, slots, edge, edge), lambda r, *_: (r, 0, 0, 0)),
                pl.BlockSpec((width, edge), lambda r, *_: (0, r)),
            ],
            out_specs=pl.BlockSpec(memory_space=pltpu.VMEM),
            scratch_shapes=[pltpu.VMEM((entries, width, edge), jnp.float32)],
        ),
        compiler_params=pltpu.CompilerParams(vmem_limit_bytes=VMEM_BYTES),
        name="project_terms",
    )(live, slot_entry, blocks, basis)


def owner_sum_kernel(goal_ref, incoming_ref, out_ref, total):
    edge = incoming_ref.shape[-1]

    @pl.loop(0, total.shape[0])
    def _(b):
        total[b] = jnp.zeros(total.shape[1:], total.dtype)

    @pl.loop(0, incoming_ref.shape[0])
    def _(i):
        total[goal_ref[i]] += incoming_ref[i].astype(jnp.float32)

    for b in range(total.shape[0]):
        out_ref[:, b * edge : (b + 1) * edge] = total[b].astype(out_ref.dtype)


def owner_sum(goal, incoming, owned_blocks):
    _, width, edge = incoming.shape
    return pl.pallas_call(
        owner_sum_kernel,
        out_shape=jax.ShapeDtypeStruct((width, owned_blocks * edge), jnp.bfloat16),
        in_specs=[
            pl.BlockSpec(memory_space=pltpu.SMEM),
            pl.BlockSpec(memory_space=pltpu.VMEM),
        ],
        out_specs=pl.BlockSpec(memory_space=pltpu.VMEM),
        scratch_shapes=[pltpu.VMEM((owned_blocks, width, edge), jnp.float32)],
        compiler_params=pltpu.CompilerParams(vmem_limit_bytes=VMEM_BYTES),
        name="owner_sum",
    )(goal, incoming)


MESH = pl.DeviceIdType.MESH


def greet_docs():
    owners, me, core = lax.axis_size("docs"), lax.axis_index("docs"), lax.axis_index("cols")
    barrier = pltpu.get_barrier_semaphore()

    @pl.loop(1, owners)
    def _(k):
        peer = lax.rem(me + k, owners)
        pl.semaphore_signal(barrier, inc=1, device_id=(peer, core), device_id_type=MESH)

    pl.semaphore_wait(barrier, owners - 1)


def exchange_kernel(x_ref, out_ref, send_sem, recv_sem, own_sem):
    owners, me, core = lax.axis_size("docs"), lax.axis_index("docs"), lax.axis_index("cols")
    greet_docs()

    def transfer(k):
        peer = lax.rem(me + k, owners)
        return pltpu.make_async_remote_copy(
            src_ref=x_ref.at[peer], dst_ref=out_ref.at[me],
            send_sem=send_sem.at[k], recv_sem=recv_sem.at[k],
            device_id=(peer, core), device_id_type=MESH,
        )

    @pl.loop(1, owners)
    def _(k):
        transfer(k).start()

    own = pltpu.make_async_copy(x_ref.at[me], out_ref.at[me], own_sem)
    own.start()
    own.wait()

    @pl.loop(1, owners)
    def _(k):
        transfer(k).wait()


def exchange(value, collective_id, space, name):
    owners = lax.axis_size("docs")
    return pl.pallas_call(
        exchange_kernel,
        out_shape=jax.ShapeDtypeStruct(value.shape, value.dtype),
        in_specs=[pl.BlockSpec(memory_space=space)],
        out_specs=pl.BlockSpec(memory_space=space),
        scratch_shapes=[
            pltpu.SemaphoreType.DMA((owners,)),
            pltpu.SemaphoreType.DMA((owners,)),
            pltpu.SemaphoreType.DMA,
        ],
        compiler_params=pltpu.CompilerParams(collective_id=collective_id, has_side_effects=True),
        name=name,
    )(value)


def gram_sum_kernel(x_ref, out_ref, arrived, send_sem, recv_sem, send_all, recv_all):
    owners, cores = lax.axis_size("docs"), lax.axis_size("cols")
    me, core = lax.axis_index("docs"), lax.axis_index("cols")
    ranks = owners * cores
    rank = me * cores + core
    barrier = pltpu.get_barrier_semaphore()

    @pl.loop(1, ranks)
    def _(k):
        peer = lax.rem(rank + k, ranks)
        pl.semaphore_signal(
            barrier, inc=1, device_id=(peer // cores, lax.rem(peer, cores)), device_id_type=MESH
        )

    pl.semaphore_wait(barrier, ranks - 1)

    def part(k):
        peer = lax.rem(me + k, owners)
        return pltpu.make_async_remote_copy(
            src_ref=x_ref.at[peer * cores + core], dst_ref=arrived.at[k],
            send_sem=send_sem.at[k], recv_sem=recv_sem.at[k],
            device_id=(peer, core), device_id_type=MESH,
        )

    def result(k):
        peer = lax.rem(rank + k, ranks)
        return pltpu.make_async_remote_copy(
            src_ref=out_ref.at[rank], dst_ref=out_ref.at[rank],
            send_sem=send_all.at[k], recv_sem=recv_all.at[k],
            device_id=(peer // cores, lax.rem(peer, cores)), device_id_type=MESH,
        )

    @pl.loop(1, owners)
    def _(k):
        part(k).start()

    @pl.loop(1, owners)
    def _(k):
        part(k).wait()

    out_ref[rank] = lax.fori_loop(
        1, owners, lambda k, total: total + arrived[k], x_ref[rank]
    )

    @pl.loop(1, ranks)
    def _(k):
        result(k).start()

    @pl.loop(1, ranks)
    def _(k):
        result(k).wait()


def gram_sum(gram):
    owners, ranks = lax.axis_size("docs"), lax.axis_size("docs") * lax.axis_size("cols")
    lanes = 128
    parts = gram.reshape(ranks, gram.size // (ranks * lanes), lanes)
    summed = pl.pallas_call(
        gram_sum_kernel,
        out_shape=jax.ShapeDtypeStruct(parts.shape, parts.dtype),
        in_specs=[pl.BlockSpec(memory_space=pltpu.VMEM)],
        out_specs=pl.BlockSpec(memory_space=pltpu.VMEM),
        scratch_shapes=[
            pltpu.VMEM((owners,) + parts.shape[1:], parts.dtype),
            pltpu.SemaphoreType.DMA((owners,)),
            pltpu.SemaphoreType.DMA((owners,)),
            pltpu.SemaphoreType.DMA((ranks,)),
            pltpu.SemaphoreType.DMA((ranks,)),
        ],
        compiler_params=pltpu.CompilerParams(collective_id=3, has_side_effects=True),
        name="gram_sum",
    )(parts)
    return summed.reshape(gram.shape)


PANEL = 32


def inverse_factor_kernel(gram_ref, out_ref, work):
    size = gram_ref.shape[0]
    work[:, :size] = gram_ref[...]
    rows = lax.broadcasted_iota(jnp.int32, (size, size), 0)
    lanes = lax.broadcasted_iota(jnp.int32, (size, size), 1)
    work[:, size:] = (rows == lanes).astype(jnp.float32)
    row_at = lax.broadcasted_iota(jnp.int32, (PANEL, 1), 0)
    for first in range(0, size, PANEL):
        low = first // 128 * 128
        high = size + low + 128
        panel = work[first : first + PANEL, low:high]
        for j in range(PANEL):
            at = first - low + j
            column = panel[:, at : at + 1]
            pivot = column[j : j + 1]
            scale = lax.rsqrt(pivot)
            scale = scale * (1.5 - 0.5 * pivot * scale * scale)
            row = panel[j : j + 1] * scale
            factor = jnp.where(row_at > j, column * scale, 0.0)
            panel = jnp.where(row_at == j, row, panel - factor * row)
        out_ref[first : first + PANEL, : low + 128] = panel[:, size - low :]
        if low + 128 < size:
            out_ref[first : first + PANEL, low + 128 :] = jnp.zeros(
                (PANEL, size - low - 128), jnp.float32
            )
        below = first + PANEL
        if below < size:
            upper = panel[:, : size - low]
            change = lax.dot_general(
                upper, panel, (((0,), (0,)), ((), ())),
                precision=lax.Precision.HIGHEST, preferred_element_type=jnp.float32,
            )
            work[below:, low:high] -= change[below - low :]


def inverse_factor(gram):
    size = gram.shape[0]
    return pl.pallas_call(
        inverse_factor_kernel,
        out_shape=jax.ShapeDtypeStruct(gram.shape, jnp.float32),
        in_specs=[pl.BlockSpec(memory_space=pltpu.VMEM)],
        out_specs=pl.BlockSpec(memory_space=pltpu.VMEM),
        scratch_shapes=[pltpu.VMEM((size, 2 * size), jnp.float32)],
        name="inverse_factor",
    )(gram)


def on_device(blocks, slot_entry, ghost_table, live_counts, test_matrix):
    block_rows, slot_count, block_edge, _ = blocks.shape
    sketch_width = test_matrix.shape[1]
    owners = lax.axis_size("docs")
    table = ghost_table.reshape(owners, ghost_table.shape[-1])
    per_owner = table.shape[1]
    entries = owners * per_owner
    live = live_counts.reshape(block_rows)
    padded = jnp.pad(table[:, None, :], ((0, 0), (0, 0), (0, 128 - per_owner)))
    requests = exchange(padded, 0, pltpu.VMEM, "requests")[:, 0, :per_owner]
    local_pieces = test_matrix.reshape(-1, block_edge, sketch_width)
    fetched = exchange(local_pieces[requests], 1, pl.ANY, "fetch")
    fetched = fetched.reshape(entries, block_edge, sketch_width)

    terms = sketch_terms(live, slot_entry, blocks, fetched)
    sketch = terms + lax.ppermute(terms, "cols", [(0, 1), (1, 0)])
    inverse = inverse_factor(gram_sum(gram_of(sketch)))
    basis_rows = lax.dot_general(
        sketch, inverse, (((1,), (1,)), ((), ())), precision=lax.Precision.HIGHEST
    ).astype(jnp.bfloat16)
    basis = basis_rows.T

    outgoing = project_terms(live, slot_entry, blocks, basis, entries)
    incoming = exchange(
        outgoing.reshape(owners, per_owner, sketch_width, block_edge), 2, pl.ANY, "giveback"
    )
    projected = owner_sum(
        requests.reshape(-1),
        incoming.reshape(-1, sketch_width, block_edge),
        test_matrix.shape[0] // block_edge,
    )
    return (basis_rows, projected)


def solution(mesh):
    in_specs = (
        P("docs", "cols", None, None),
        P("docs", "cols"),
        P("docs", "cols", None, None),
        P("docs", "cols"),
        P(("docs", "cols"), None),
    )
    out_specs = (P("docs", None), P(None, ("docs", "cols")))
    return jax.shard_map(
        on_device, mesh=mesh, in_specs=in_specs, out_specs=out_specs, check_vma=False
    )
```

```python
import jax
import jax.numpy as jnp
from jax import lax
from jax.experimental import pallas as pl
from jax.experimental.pallas import tpu as pltpu
from jax.sharding import PartitionSpec as P

VMEM_BYTES = 60 * 1024 * 1024
def gram_of(rows_block):
    return lax.dot_general(
        rows_block, rows_block, (((0,), (0,)), ((), ())), precision=lax.Precision.HIGHEST
    )


def place_kernel(live_ref, entry_ref, blocks_ref, out_ref):
    row = pl.program_id(0)
    edge = blocks_ref.shape[-1]
    per_owner = out_ref.shape[-1] // edge

    @pl.loop(0, out_ref.shape[0])
    def _(o):
        out_ref[o] = jnp.zeros(out_ref.shape[1:], out_ref.dtype)

    @pl.loop(0, live_ref[row])
    def _(k):
        entry = entry_ref[row, k]
        lane = pl.multiple_of(lax.rem(entry, per_owner) * edge, edge)
        out_ref[lax.div(entry, per_owner), :, pl.ds(lane, edge)] = blocks_ref[0, k]


def place_blocks(live, slot_entry, blocks, owners, per_owner):
    block_rows, slots, edge, _ = blocks.shape
    shape = (owners, block_rows * edge, per_owner * edge)
    return pl.pallas_call(
        place_kernel,
        out_shape=jax.ShapeDtypeStruct(shape, blocks.dtype),
        grid_spec=pltpu.PrefetchScalarGridSpec(
            num_scalar_prefetch=2,
            grid=(block_rows,),
            in_specs=[pl.BlockSpec((1, slots, edge, edge), lambda r, *_: (r, 0, 0, 0))],
            out_specs=pl.BlockSpec((owners, edge, per_owner * edge), lambda r, *_: (0, r, 0)),
        ),
        compiler_params=pltpu.CompilerParams(vmem_limit_bytes=VMEM_BYTES),
        cost_estimate=pl.CostEstimate(
            flops=0, transcendentals=0, bytes_accessed=2 * (blocks.size + shape[0] * shape[1] * shape[2])
        ),
        name="place_blocks",
    )(live, slot_entry, blocks)


def sketch_kernel(placed_ref, pieces_ref, out_ref):
    @pl.when(pl.program_id(0) == 0)
    def _():
        out_ref[...] = jnp.zeros_like(out_ref)

    out_ref[...] += jnp.dot(placed_ref[0], pieces_ref[0], preferred_element_type=jnp.float32)


def sketch_terms(placed, pieces):
    owners, rows, depth = placed.shape
    width = pieces.shape[-1]
    return pl.pallas_call(
        sketch_kernel,
        out_shape=jax.ShapeDtypeStruct((rows, width), jnp.float32),
        grid=(owners,),
        in_specs=[
            pl.BlockSpec((1, rows, depth), lambda o: (o, 0, 0)),
            pl.BlockSpec((1, depth, width), lambda o: (o, 0, 0)),
        ],
        out_specs=pl.BlockSpec((rows, width), lambda o: (0, 0)),
        compiler_params=pltpu.CompilerParams(vmem_limit_bytes=VMEM_BYTES),
        name="sketch_terms",
    )(placed, pieces)


def owner_sum_kernel(goal_ref, incoming_ref, out_ref, total):
    edge = total.shape[-1]
    per_owner = incoming_ref.shape[-1] // edge

    @pl.loop(0, total.shape[0])
    def _(b):
        total[b] = jnp.zeros(total.shape[1:], total.dtype)

    @pl.loop(0, incoming_ref.shape[0])
    def _(o):
        for j in range(per_owner):
            part = incoming_ref[o, :, j * edge : (j + 1) * edge]
            total[goal_ref[o * per_owner + j]] += part.astype(jnp.float32)

    for b in range(total.shape[0]):
        out_ref[:, b * edge : (b + 1) * edge] = total[b].astype(out_ref.dtype)


def owner_sum(goal, incoming, owned_blocks, edge):
    _, width, _ = incoming.shape
    return pl.pallas_call(
        owner_sum_kernel,
        out_shape=jax.ShapeDtypeStruct((width, owned_blocks * edge), jnp.bfloat16),
        in_specs=[
            pl.BlockSpec(memory_space=pltpu.SMEM),
            pl.BlockSpec(memory_space=pltpu.VMEM),
        ],
        out_specs=pl.BlockSpec(memory_space=pltpu.VMEM),
        scratch_shapes=[pltpu.VMEM((owned_blocks, width, edge), jnp.float32)],
        compiler_params=pltpu.CompilerParams(vmem_limit_bytes=VMEM_BYTES),
        name="owner_sum",
    )(goal, incoming)


MESH = pl.DeviceIdType.MESH


def greet_docs():
    owners, me, core = lax.axis_size("docs"), lax.axis_index("docs"), lax.axis_index("cols")
    barrier = pltpu.get_barrier_semaphore()

    @pl.loop(1, owners)
    def _(k):
        peer = lax.rem(me + k, owners)
        pl.semaphore_signal(barrier, inc=1, device_id=(peer, core), device_id_type=MESH)

    pl.semaphore_wait(barrier, owners - 1)


def exchange_kernel(x_ref, out_ref, send_sem, recv_sem, own_sem):
    owners, me, core = lax.axis_size("docs"), lax.axis_index("docs"), lax.axis_index("cols")
    greet_docs()

    def transfer(k):
        peer = lax.rem(me + k, owners)
        return pltpu.make_async_remote_copy(
            src_ref=x_ref.at[peer], dst_ref=out_ref.at[me],
            send_sem=send_sem.at[k], recv_sem=recv_sem.at[k],
            device_id=(peer, core), device_id_type=MESH,
        )

    @pl.loop(1, owners)
    def _(k):
        transfer(k).start()

    own = pltpu.make_async_copy(x_ref.at[me], out_ref.at[me], own_sem)
    own.start()
    own.wait()

    @pl.loop(1, owners)
    def _(k):
        transfer(k).wait()


def exchange(value, collective_id, space, name):
    owners = lax.axis_size("docs")
    return pl.pallas_call(
        exchange_kernel,
        out_shape=jax.ShapeDtypeStruct(value.shape, value.dtype),
        in_specs=[pl.BlockSpec(memory_space=space)],
        out_specs=pl.BlockSpec(memory_space=space),
        scratch_shapes=[
            pltpu.SemaphoreType.DMA((owners,)),
            pltpu.SemaphoreType.DMA((owners,)),
            pltpu.SemaphoreType.DMA,
        ],
        compiler_params=pltpu.CompilerParams(collective_id=collective_id, has_side_effects=True),
        name=name,
    )(value)


def partner(me, k, owners):
    total, bit = 0, 1
    while bit < owners:
        total = total + lax.rem(lax.div(me, bit) + lax.div(k, bit), 2) * bit
        bit *= 2
    return total


def project_kernel(basis_ref, placed_ref, out_ref, chunk, stage, chunk_sem, send_sem, recv_sem, own_sem):
    owners, me, core = lax.axis_size("docs"), lax.axis_index("docs"), lax.axis_index("cols")
    greet_docs()

    def offset(i):
        return lax.rem(i + owners // 2, owners)

    def load(i):
        slot = lax.rem(i, 2)
        peer = partner(me, offset(i), owners)
        return pltpu.make_async_copy(placed_ref.at[peer], chunk.at[slot], chunk_sem.at[slot])

    def send(k):
        peer = partner(me, k, owners)
        return pltpu.make_async_remote_copy(
            src_ref=stage.at[peer], dst_ref=out_ref.at[me],
            send_sem=send_sem.at[k], recv_sem=recv_sem.at[k],
            device_id=(peer, core), device_id_type=MESH,
        )

    own = pltpu.make_async_copy(stage.at[me], out_ref.at[me], own_sem)
    load(jnp.int32(0)).start()

    @pl.loop(0, owners)
    def _(i):
        @pl.when(i + 1 < owners)
        def _():
            load(i + 1).start()

        load(i).wait()
        k = offset(i)
        stage[partner(me, k, owners)] = jnp.dot(
            basis_ref[...], chunk[lax.rem(i, 2)], preferred_element_type=jnp.float32
        ).astype(stage.dtype)

        @pl.when(k != 0)
        def _():
            send(k).start()

        @pl.when(k == 0)
        def _():
            own.start()

    own.wait()

    @pl.loop(1, owners)
    def _(k):
        send(k).wait()


def project_terms(basis, placed):
    owners, rows, depth = placed.shape
    width = basis.shape[0]
    shape = (owners, width, depth)
    return pl.pallas_call(
        project_kernel,
        out_shape=jax.ShapeDtypeStruct(shape, jnp.bfloat16),
        in_specs=[pl.BlockSpec(memory_space=pltpu.VMEM), pl.BlockSpec(memory_space=pl.ANY)],
        out_specs=pl.BlockSpec(memory_space=pl.ANY),
        scratch_shapes=[
            pltpu.VMEM((2, rows, depth), jnp.bfloat16),
            pltpu.VMEM(shape, jnp.bfloat16),
            pltpu.SemaphoreType.DMA((2,)),
            pltpu.SemaphoreType.DMA((owners,)),
            pltpu.SemaphoreType.DMA((owners,)),
            pltpu.SemaphoreType.DMA,
        ],
        compiler_params=pltpu.CompilerParams(
            collective_id=2, has_side_effects=True, vmem_limit_bytes=VMEM_BYTES
        ),
        name="project_terms",
    )(basis, placed)


def gram_sum_kernel(x_ref, out_ref, arrived, send_sem, recv_sem, send_all, recv_all):
    owners, cores = lax.axis_size("docs"), lax.axis_size("cols")
    me, core = lax.axis_index("docs"), lax.axis_index("cols")
    ranks = owners * cores
    rank = me * cores + core
    barrier = pltpu.get_barrier_semaphore()

    @pl.loop(1, ranks)
    def _(k):
        peer = lax.rem(rank + k, ranks)
        pl.semaphore_signal(
            barrier, inc=1, device_id=(peer // cores, lax.rem(peer, cores)), device_id_type=MESH
        )

    pl.semaphore_wait(barrier, ranks - 1)

    def part(k):
        peer = lax.rem(me + k, owners)
        return pltpu.make_async_remote_copy(
            src_ref=x_ref.at[peer * cores + core], dst_ref=arrived.at[k],
            send_sem=send_sem.at[k], recv_sem=recv_sem.at[k],
            device_id=(peer, core), device_id_type=MESH,
        )

    def result(k):
        peer = lax.rem(rank + k, ranks)
        return pltpu.make_async_remote_copy(
            src_ref=out_ref.at[rank], dst_ref=out_ref.at[rank],
            send_sem=send_all.at[k], recv_sem=recv_all.at[k],
            device_id=(peer // cores, lax.rem(peer, cores)), device_id_type=MESH,
        )

    @pl.loop(1, owners)
    def _(k):
        part(k).start()

    @pl.loop(1, owners)
    def _(k):
        part(k).wait()

    out_ref[rank] = lax.fori_loop(
        1, owners, lambda k, total: total + arrived[k], x_ref[rank]
    )

    @pl.loop(1, ranks)
    def _(k):
        result(k).start()

    @pl.loop(1, ranks)
    def _(k):
        result(k).wait()


def gram_sum(gram):
    owners, ranks = lax.axis_size("docs"), lax.axis_size("docs") * lax.axis_size("cols")
    lanes = 128
    parts = gram.reshape(ranks, gram.size // (ranks * lanes), lanes)
    summed = pl.pallas_call(
        gram_sum_kernel,
        out_shape=jax.ShapeDtypeStruct(parts.shape, parts.dtype),
        in_specs=[pl.BlockSpec(memory_space=pltpu.VMEM)],
        out_specs=pl.BlockSpec(memory_space=pltpu.VMEM),
        scratch_shapes=[
            pltpu.VMEM((owners,) + parts.shape[1:], parts.dtype),
            pltpu.SemaphoreType.DMA((owners,)),
            pltpu.SemaphoreType.DMA((owners,)),
            pltpu.SemaphoreType.DMA((ranks,)),
            pltpu.SemaphoreType.DMA((ranks,)),
        ],
        compiler_params=pltpu.CompilerParams(collective_id=3, has_side_effects=True),
        name="gram_sum",
    )(parts)
    return summed.reshape(gram.shape)


PANEL = 32


def inverse_factor_kernel(gram_ref, out_ref, work):
    size = gram_ref.shape[0]
    work[:, :size] = gram_ref[...]
    rows = lax.broadcasted_iota(jnp.int32, (size, size), 0)
    lanes = lax.broadcasted_iota(jnp.int32, (size, size), 1)
    work[:, size:] = (rows == lanes).astype(jnp.float32)
    row_at = lax.broadcasted_iota(jnp.int32, (PANEL, 1), 0)
    for first in range(0, size, PANEL):
        low = first // 128 * 128
        high = size + low + 128
        panel = work[first : first + PANEL, low:high]
        for j in range(PANEL):
            at = first - low + j
            column = panel[:, at : at + 1]
            pivot = column[j : j + 1]
            scale = lax.rsqrt(pivot)
            scale = scale * (1.5 - 0.5 * pivot * scale * scale)
            row = panel[j : j + 1] * scale
            factor = jnp.where(row_at > j, column * scale, 0.0)
            panel = jnp.where(row_at == j, row, panel - factor * row)
        out_ref[first : first + PANEL, : low + 128] = panel[:, size - low :]
        if low + 128 < size:
            out_ref[first : first + PANEL, low + 128 :] = jnp.zeros(
                (PANEL, size - low - 128), jnp.float32
            )
        below = first + PANEL
        if below < size:
            upper = panel[:, : size - low]
            change = lax.dot_general(
                upper, panel, (((0,), (0,)), ((), ())),
                precision=lax.Precision.HIGHEST, preferred_element_type=jnp.float32,
            )
            work[below:, low:high] -= change[below - low :]


def inverse_factor(gram):
    size = gram.shape[0]
    return pl.pallas_call(
        inverse_factor_kernel,
        out_shape=jax.ShapeDtypeStruct(gram.shape, jnp.float32),
        in_specs=[pl.BlockSpec(memory_space=pltpu.VMEM)],
        out_specs=pl.BlockSpec(memory_space=pltpu.VMEM),
        scratch_shapes=[pltpu.VMEM((size, 2 * size), jnp.float32)],
        name="inverse_factor",
    )(gram)


def on_device(blocks, slot_entry, ghost_table, live_counts, test_matrix):
    block_rows, slot_count, block_edge, _ = blocks.shape
    sketch_width = test_matrix.shape[1]
    owners = lax.axis_size("docs")
    table = ghost_table.reshape(owners, ghost_table.shape[-1])
    per_owner = table.shape[1]
    live = live_counts.reshape(block_rows)
    padded = jnp.pad(table[:, None, :], ((0, 0), (0, 0), (0, 128 - per_owner)))
    requests = exchange(padded, 0, pltpu.VMEM, "requests")[:, 0, :per_owner]
    local_pieces = test_matrix.reshape(-1, block_edge, sketch_width)
    fetched = lax.all_to_all(
        local_pieces[requests], "docs", split_axis=0, concat_axis=0, tiled=True
    )
    pieces = fetched.reshape(owners, per_owner * block_edge, sketch_width)
    placed = place_blocks(live, slot_entry, blocks, owners, per_owner)

    terms = sketch_terms(placed, pieces)
    sketch = terms + lax.ppermute(terms, "cols", [(0, 1), (1, 0)])
    inverse = inverse_factor(gram_sum(gram_of(sketch)))
    basis_rows = lax.dot_general(
        sketch, inverse, (((1,), (1,)), ((), ())), precision=lax.Precision.HIGHEST
    ).astype(jnp.bfloat16)
    basis = basis_rows.T

    incoming = project_terms(basis, placed)
    projected = owner_sum(
        requests.reshape(-1), incoming, test_matrix.shape[0] // block_edge, block_edge
    )
    return (basis_rows, projected)


def solution(mesh):
    in_specs = (
        P("docs", "cols", None, None),
        P("docs", "cols"),
        P("docs", "cols", None, None),
        P("docs", "cols"),
        P(("docs", "cols"), None),
    )
    out_specs = (P("docs", None), P(None, ("docs", "cols")))
    return jax.shard_map(
        on_device, mesh=mesh, in_specs=in_specs, out_specs=out_specs, check_vma=False
    )
```

```python
import jax
import jax.numpy as jnp
from jax import lax
from jax.experimental import pallas as pl
from jax.experimental.pallas import tpu as pltpu
from jax.sharding import PartitionSpec as P

VMEM_BYTES = 60 * 1024 * 1024
SKETCH_ROWS = 256
def gram_of(rows_block):
    return lax.dot_general(
        rows_block, rows_block, (((0,), (0,)), ((), ())), precision=lax.Precision.HIGHEST
    )


def place_kernel(live_ref, entry_ref, blocks_ref, out_ref):
    row = pl.program_id(0)
    edge = blocks_ref.shape[-1]
    per_owner = out_ref.shape[-1] // edge

    @pl.loop(0, out_ref.shape[0])
    def _(o):
        out_ref[o] = jnp.zeros(out_ref.shape[1:], out_ref.dtype)

    @pl.loop(0, live_ref[row])
    def _(k):
        entry = entry_ref[row, k]
        lane = pl.multiple_of(lax.rem(entry, per_owner) * edge, edge)
        out_ref[lax.div(entry, per_owner), :, pl.ds(lane, edge)] = blocks_ref[0, k]


def place_blocks(live, slot_entry, blocks, owners, per_owner):
    block_rows, slots, edge, _ = blocks.shape
    shape = (owners, block_rows * edge, per_owner * edge)
    return pl.pallas_call(
        place_kernel,
        out_shape=jax.ShapeDtypeStruct(shape, blocks.dtype),
        grid_spec=pltpu.PrefetchScalarGridSpec(
            num_scalar_prefetch=2,
            grid=(block_rows,),
            in_specs=[pl.BlockSpec((1, slots, edge, edge), lambda r, *_: (r, 0, 0, 0))],
            out_specs=pl.BlockSpec((owners, edge, per_owner * edge), lambda r, *_: (0, r, 0)),
        ),
        compiler_params=pltpu.CompilerParams(vmem_limit_bytes=VMEM_BYTES),
        cost_estimate=pl.CostEstimate(
            flops=0, transcendentals=0, bytes_accessed=2 * (blocks.size + shape[0] * shape[1] * shape[2])
        ),
        name="place_blocks",
    )(live, slot_entry, blocks)


def sketch_kernel(placed_ref, pieces_ref, out_ref):
    out_ref[...] = sum(
        jnp.dot(placed_ref[o], pieces_ref[o], preferred_element_type=jnp.float32)
        for o in range(placed_ref.shape[0])
    )


def sketch_terms(placed, pieces):
    owners, rows, depth = placed.shape
    width = pieces.shape[-1]
    return pl.pallas_call(
        sketch_kernel,
        out_shape=jax.ShapeDtypeStruct((rows, width), jnp.float32),
        grid=(rows // SKETCH_ROWS,),
        in_specs=[
            pl.BlockSpec((owners, SKETCH_ROWS, depth), lambda r: (0, r, 0)),
            pl.BlockSpec(memory_space=pltpu.VMEM),
        ],
        out_specs=pl.BlockSpec((SKETCH_ROWS, width), lambda r: (r, 0)),
        compiler_params=pltpu.CompilerParams(vmem_limit_bytes=VMEM_BYTES),
        name="sketch_terms",
    )(placed, pieces)


def owner_sum_kernel(goal_ref, incoming_ref, out_ref, total):
    edge = total.shape[-1]
    per_owner = incoming_ref.shape[-1] // edge

    @pl.loop(0, total.shape[0])
    def _(b):
        total[b] = jnp.zeros(total.shape[1:], total.dtype)

    @pl.loop(0, incoming_ref.shape[0])
    def _(o):
        for j in range(per_owner):
            part = incoming_ref[o, :, j * edge : (j + 1) * edge]
            total[goal_ref[o * per_owner + j]] += part.astype(jnp.float32)

    for b in range(total.shape[0]):
        out_ref[:, b * edge : (b + 1) * edge] = total[b].astype(out_ref.dtype)


def owner_sum(goal, incoming, owned_blocks, edge):
    _, width, _ = incoming.shape
    return pl.pallas_call(
        owner_sum_kernel,
        out_shape=jax.ShapeDtypeStruct((width, owned_blocks * edge), jnp.bfloat16),
        in_specs=[
            pl.BlockSpec(memory_space=pltpu.SMEM),
            pl.BlockSpec(memory_space=pltpu.VMEM),
        ],
        out_specs=pl.BlockSpec(memory_space=pltpu.VMEM),
        scratch_shapes=[pltpu.VMEM((owned_blocks, width, edge), jnp.float32)],
        compiler_params=pltpu.CompilerParams(vmem_limit_bytes=VMEM_BYTES),
        name="owner_sum",
    )(goal, incoming)


MESH = pl.DeviceIdType.MESH


def greet_docs():
    owners, me, core = lax.axis_size("docs"), lax.axis_index("docs"), lax.axis_index("cols")
    barrier = pltpu.get_barrier_semaphore()

    @pl.loop(1, owners)
    def _(k):
        peer = lax.rem(me + k, owners)
        pl.semaphore_signal(barrier, inc=1, device_id=(peer, core), device_id_type=MESH)

    pl.semaphore_wait(barrier, owners - 1)


def exchange_kernel(x_ref, out_ref, send_sem, recv_sem, own_sem):
    owners, me, core = lax.axis_size("docs"), lax.axis_index("docs"), lax.axis_index("cols")
    greet_docs()

    def transfer(k):
        peer = lax.rem(me + k, owners)
        return pltpu.make_async_remote_copy(
            src_ref=x_ref.at[peer], dst_ref=out_ref.at[me],
            send_sem=send_sem.at[k], recv_sem=recv_sem.at[k],
            device_id=(peer, core), device_id_type=MESH,
        )

    @pl.loop(1, owners)
    def _(k):
        transfer(k).start()

    own = pltpu.make_async_copy(x_ref.at[me], out_ref.at[me], own_sem)
    own.start()
    own.wait()

    @pl.loop(1, owners)
    def _(k):
        transfer(k).wait()


def exchange(value, collective_id, space, name):
    owners = lax.axis_size("docs")
    return pl.pallas_call(
        exchange_kernel,
        out_shape=jax.ShapeDtypeStruct(value.shape, value.dtype),
        in_specs=[pl.BlockSpec(memory_space=space)],
        out_specs=pl.BlockSpec(memory_space=space),
        scratch_shapes=[
            pltpu.SemaphoreType.DMA((owners,)),
            pltpu.SemaphoreType.DMA((owners,)),
            pltpu.SemaphoreType.DMA,
        ],
        compiler_params=pltpu.CompilerParams(collective_id=collective_id, has_side_effects=True),
        name=name,
    )(value)


def partner(me, k, owners):
    total, bit = 0, 1
    while bit < owners:
        total = total + lax.rem(lax.div(me, bit) + lax.div(k, bit), 2) * bit
        bit *= 2
    return total


def project_kernel(basis_ref, placed_ref, out_ref, chunk, stage, chunk_sem, send_sem, recv_sem, own_sem):
    owners, me, core = lax.axis_size("docs"), lax.axis_index("docs"), lax.axis_index("cols")
    greet_docs()

    def offset(i):
        return lax.rem(i + owners // 2, owners)

    def load(i):
        slot = lax.rem(i, 2)
        peer = partner(me, offset(i), owners)
        return pltpu.make_async_copy(placed_ref.at[peer], chunk.at[slot], chunk_sem.at[slot])

    def send(k):
        peer = partner(me, k, owners)
        return pltpu.make_async_remote_copy(
            src_ref=stage.at[peer], dst_ref=out_ref.at[me],
            send_sem=send_sem.at[k], recv_sem=recv_sem.at[k],
            device_id=(peer, core), device_id_type=MESH,
        )

    own = pltpu.make_async_copy(stage.at[me], out_ref.at[me], own_sem)
    load(jnp.int32(0)).start()

    @pl.loop(0, owners)
    def _(i):
        @pl.when(i + 1 < owners)
        def _():
            load(i + 1).start()

        load(i).wait()
        k = offset(i)
        stage[partner(me, k, owners)] = jnp.dot(
            basis_ref[...], chunk[lax.rem(i, 2)], preferred_element_type=jnp.float32
        ).astype(stage.dtype)

        @pl.when(k != 0)
        def _():
            send(k).start()

        @pl.when(k == 0)
        def _():
            own.start()

    own.wait()

    @pl.loop(1, owners)
    def _(k):
        send(k).wait()


def project_terms(basis, placed):
    owners, rows, depth = placed.shape
    width = basis.shape[0]
    shape = (owners, width, depth)
    return pl.pallas_call(
        project_kernel,
        out_shape=jax.ShapeDtypeStruct(shape, jnp.bfloat16),
        in_specs=[pl.BlockSpec(memory_space=pltpu.VMEM), pl.BlockSpec(memory_space=pl.ANY)],
        out_specs=pl.BlockSpec(memory_space=pl.ANY),
        scratch_shapes=[
            pltpu.VMEM((2, rows, depth), jnp.bfloat16),
            pltpu.VMEM(shape, jnp.bfloat16),
            pltpu.SemaphoreType.DMA((2,)),
            pltpu.SemaphoreType.DMA((owners,)),
            pltpu.SemaphoreType.DMA((owners,)),
            pltpu.SemaphoreType.DMA,
        ],
        compiler_params=pltpu.CompilerParams(
            collective_id=2, has_side_effects=True, vmem_limit_bytes=VMEM_BYTES
        ),
        name="project_terms",
    )(basis, placed)


def gram_sum_kernel(x_ref, out_ref, arrived, send_sem, recv_sem, send_all, recv_all):
    owners, cores = lax.axis_size("docs"), lax.axis_size("cols")
    me, core = lax.axis_index("docs"), lax.axis_index("cols")
    ranks = owners * cores
    rank = me * cores + core
    barrier = pltpu.get_barrier_semaphore()

    @pl.loop(1, ranks)
    def _(k):
        peer = lax.rem(rank + k, ranks)
        pl.semaphore_signal(
            barrier, inc=1, device_id=(peer // cores, lax.rem(peer, cores)), device_id_type=MESH
        )

    pl.semaphore_wait(barrier, ranks - 1)

    def part(k):
        peer = lax.rem(me + k, owners)
        return pltpu.make_async_remote_copy(
            src_ref=x_ref.at[peer * cores + core], dst_ref=arrived.at[k],
            send_sem=send_sem.at[k], recv_sem=recv_sem.at[k],
            device_id=(peer, core), device_id_type=MESH,
        )

    def result(k):
        peer = lax.rem(rank + k, ranks)
        return pltpu.make_async_remote_copy(
            src_ref=out_ref.at[rank], dst_ref=out_ref.at[rank],
            send_sem=send_all.at[k], recv_sem=recv_all.at[k],
            device_id=(peer // cores, lax.rem(peer, cores)), device_id_type=MESH,
        )

    @pl.loop(1, owners)
    def _(k):
        part(k).start()

    @pl.loop(1, owners)
    def _(k):
        part(k).wait()

    out_ref[rank] = lax.fori_loop(
        1, owners, lambda k, total: total + arrived[k], x_ref[rank]
    )

    @pl.loop(1, ranks)
    def _(k):
        result(k).start()

    @pl.loop(1, ranks)
    def _(k):
        result(k).wait()


def gram_sum(gram):
    owners, ranks = lax.axis_size("docs"), lax.axis_size("docs") * lax.axis_size("cols")
    lanes = 128
    parts = gram.reshape(ranks, gram.size // (ranks * lanes), lanes)
    summed = pl.pallas_call(
        gram_sum_kernel,
        out_shape=jax.ShapeDtypeStruct(parts.shape, parts.dtype),
        in_specs=[pl.BlockSpec(memory_space=pltpu.VMEM)],
        out_specs=pl.BlockSpec(memory_space=pltpu.VMEM),
        scratch_shapes=[
            pltpu.VMEM((owners,) + parts.shape[1:], parts.dtype),
            pltpu.SemaphoreType.DMA((owners,)),
            pltpu.SemaphoreType.DMA((owners,)),
            pltpu.SemaphoreType.DMA((ranks,)),
            pltpu.SemaphoreType.DMA((ranks,)),
        ],
        compiler_params=pltpu.CompilerParams(collective_id=3, has_side_effects=True),
        name="gram_sum",
    )(parts)
    return summed.reshape(gram.shape)


PANEL = 32


def inverse_factor_kernel(gram_ref, out_ref, work):
    size = gram_ref.shape[0]
    work[:, :size] = gram_ref[...]
    rows = lax.broadcasted_iota(jnp.int32, (size, size), 0)
    lanes = lax.broadcasted_iota(jnp.int32, (size, size), 1)
    work[:, size:] = (rows == lanes).astype(jnp.float32)
    row_at = lax.broadcasted_iota(jnp.int32, (PANEL, 1), 0)
    for first in range(0, size, PANEL):
        low = first // 128 * 128
        high = size + low + 128
        panel = work[first : first + PANEL, low:high]
        for j in range(PANEL):
            at = first - low + j
            column = panel[:, at : at + 1]
            pivot = column[j : j + 1]
            scale = lax.rsqrt(pivot)
            scale = scale * (1.5 - 0.5 * pivot * scale * scale)
            row = panel[j : j + 1] * scale
            factor = jnp.where(row_at > j, column * scale, 0.0)
            panel = jnp.where(row_at == j, row, panel - factor * row)
        out_ref[first : first + PANEL, : low + 128] = panel[:, size - low :]
        if low + 128 < size:
            out_ref[first : first + PANEL, low + 128 :] = jnp.zeros(
                (PANEL, size - low - 128), jnp.float32
            )
        below = first + PANEL
        if below < size:
            upper = panel[:, : size - low]
            change = lax.dot_general(
                upper, panel, (((0,), (0,)), ((), ())),
                precision=lax.Precision.HIGHEST, preferred_element_type=jnp.float32,
            )
            work[below:, low:high] -= change[below - low :]


def inverse_factor(gram):
    size = gram.shape[0]
    return pl.pallas_call(
        inverse_factor_kernel,
        out_shape=jax.ShapeDtypeStruct(gram.shape, jnp.float32),
        in_specs=[pl.BlockSpec(memory_space=pltpu.VMEM)],
        out_specs=pl.BlockSpec(memory_space=pltpu.VMEM),
        scratch_shapes=[pltpu.VMEM((size, 2 * size), jnp.float32)],
        name="inverse_factor",
    )(gram)


def on_device(blocks, slot_entry, ghost_table, live_counts, test_matrix):
    block_rows, slot_count, block_edge, _ = blocks.shape
    sketch_width = test_matrix.shape[1]
    owners = lax.axis_size("docs")
    table = ghost_table.reshape(owners, ghost_table.shape[-1])
    per_owner = table.shape[1]
    live = live_counts.reshape(block_rows)
    padded = jnp.pad(table[:, None, :], ((0, 0), (0, 0), (0, 128 - per_owner)))
    requests = exchange(padded, 0, pltpu.VMEM, "requests")[:, 0, :per_owner]
    local_pieces = test_matrix.reshape(-1, block_edge, sketch_width)
    fetched = lax.all_to_all(
        local_pieces[requests], "docs", split_axis=0, concat_axis=0, tiled=True
    )
    pieces = fetched.reshape(owners, per_owner * block_edge, sketch_width)
    placed = place_blocks(live, slot_entry, blocks, owners, per_owner)

    terms = sketch_terms(placed, pieces)
    sketch = terms + lax.ppermute(terms, "cols", [(0, 1), (1, 0)])
    inverse = inverse_factor(gram_sum(gram_of(sketch)))
    basis_rows = lax.dot_general(
        sketch, inverse, (((1,), (1,)), ((), ())), precision=lax.Precision.HIGHEST
    ).astype(jnp.bfloat16)
    basis = basis_rows.T

    incoming = project_terms(basis, placed)
    projected = owner_sum(
        requests.reshape(-1), incoming, test_matrix.shape[0] // block_edge, block_edge
    )
    return (basis_rows, projected)


def solution(mesh):
    in_specs = (
        P("docs", "cols", None, None),
        P("docs", "cols"),
        P("docs", "cols", None, None),
        P("docs", "cols"),
        P(("docs", "cols"), None),
    )
    out_specs = (P("docs", None), P(None, ("docs", "cols")))
    return jax.shard_map(
        on_device, mesh=mesh, in_specs=in_specs, out_specs=out_specs, check_vma=False
    )
```
